32 devices in a mesh: freq: 4 (over y, x), blk: 8 (over z, core).
Axes of the slice: x: 2, y: 2, z: 4, core: 2. Of those that a mesh axis runs over, the one named last changes fastest.
Arguments:
- voltages: float32 [32, 32, 2, 128, 256], P('blk', None, None, 'freq'), may hold values from -6 to 6
- pair_table: int32 [528, 2], P('blk'), may hold values from 0 to 31, as said below
- bad_feeds: int32 [64], replicated, may hold values from 0 to 2047
Outputs:
- visibilities: float32 [528, 32, 2, 128, 128], P('blk', 'freq')
The draws below stay inside these ranges and needn't reach their ends.
Inputs may be any that keep to these rules, and one draw needn't show every extreme that they name: `pair_table`: device k of blk holds blocks k * 4 to k * 4 + 3 and tiles k * 66 to k * 66 + 65. Of its tiles, the first 4 (5) / 2 name two of its own blocks; then for d = 1 to 3 in turn, 16 tiles each name one own block and one block of device k + d; the last (17) / 2 name one own block and one block of device k + 4; device numbers are taken modulo 32 / 4, and either block of a tile may come first. Every unordered pair of blocks is named at least once.
All inputs are finite; a program needn't handle non-finite values.
Results may differ from the reference program's by a relative error of at most 0.000098.
Values sent between devices are 32-bit elements; how exact they have to be, the bound alone decides.
A program may use at most 320 MiB of HBM per device.

```python
import jax
import jax.numpy as jnp
from jax import lax

BI = 128
SAMP = 256
NBAD = 64
NB = 32
FEEDS = 2048
CHAN = 32
BPD = 4


def draw_pair_table(key, part):
    key = jax.random.fold_in(key, 5)
    devices = NB // BPD
    half = devices // 2
    square = BPD * BPD
    shared = (square + 1) // 2
    order_key, flip_key, turn_key, group_key = jax.random.split(key, 4)
    order = jax.random.permutation(order_key, square).astype(jnp.int32)
    flips = jax.random.randint(flip_key, (devices,), 0, 2)
    lefts = []
    rights = []
    for device in range(devices):
        base = device * BPD
        for one in range(BPD):
            for two in range(one, BPD):
                lefts.append(jnp.array([base + one], jnp.int32))
                rights.append(jnp.array([base + two], jnp.int32))
        for step in range(1, half):
            other = (device + step) % devices * BPD
            mixed = jax.random.permutation(jax.random.fold_in(group_key, device * devices + step), square).astype(jnp.int32)
            lefts.append(base + mixed // BPD)
            rights.append(other + mixed % BPD)
        lower = device % half
        upper = lower + half
        count_low = jnp.where(flips[lower] == 1, shared, square - shared)
        slot = jnp.arange(shared, dtype=jnp.int32)
        if device < half:
            pick = slot
        else:
            pick = count_low + slot
            pick = jnp.where(pick < square, pick, slot)
        tile = order[pick]
        low_block = (lower * BPD + tile // BPD).astype(jnp.int32)
        up_block = (upper * BPD + tile % BPD).astype(jnp.int32)
        if device < half:
            lefts.append(low_block)
            rights.append(up_block)
        else:
            lefts.append(up_block)
            rights.append(low_block)
    left = jnp.concatenate(lefts)
    right = jnp.concatenate(rights)
    turned = jax.random.randint(turn_key, left.shape, 0, 2) == 1
    return jnp.stack([jnp.where(turned, right, left), jnp.where(turned, left, right)], axis=1).astype(jnp.int32)


def place_ends(values, key, least, top_value):
    longest = values.shape.index(max(values.shape))
    spots = []
    for shift in (0, 1):
        where = [jax.random.randint(jax.random.fold_in(key, axis), (), 0, length) for axis, length in enumerate(values.shape)]
        where[longest] = (where[longest] + shift) % values.shape[longest]
        spots.append(tuple(where))
    return values.at[spots[0]].set(least).at[spots[1]].set(top_value)


def levels(key, dims, shards, least, top_value):
    gain = 1.0
    for dim, blocks in shards:
        draws = jax.random.uniform(jax.random.fold_in(jax.random.fold_in(key, 6), dim), (blocks,), jnp.float32, least / len(shards), top_value / len(shards))
        gain = gain * jnp.repeat(jnp.exp(draws), dims[dim] // blocks).reshape((-1,) + (1,) * (len(dims) - 1 - dim))
    return gain


def noise(stream_key, dims, deviation, bound, shards=(), kind=jnp.bfloat16):
    loudness = levels(stream_key, dims, shards, -0.22, 0.18) if shards else 1.0
    values = jax.random.normal(stream_key, dims, jnp.float32) * deviation * loudness
    return jnp.minimum(jnp.maximum(values, -bound), bound).astype(kind)


def setup_inputs(seed: int = 0) -> dict:
    keys = jax.random.split(jax.random.key(seed), 4)
    return {
        "voltages": noise(keys[0], (NB, CHAN, 2, BI, SAMP), 1.0, 6.0, ((0, 8), (3, 4)), jnp.float32),
        "pair_table": draw_pair_table(jax.random.fold_in(keys[3], 71), 0),
        "bad_feeds": place_ends(jax.random.randint(keys[2], (NBAD,), 0, FEEDS), jax.random.fold_in(keys[2], 1), 0, FEEDS - 1).astype(jnp.int32),
    }


def reference(voltages, pair_table, bad_feeds):
    inputs = jnp.arange(NB * BI, dtype=jnp.int32).reshape(NB, BI)
    flagged = jnp.any((inputs // 2)[:, :, None] == bad_feeds[None, None, :], axis=-1)
    keep = jnp.where(flagged, 0.0, 1.0).astype(jnp.float32)
    clean = voltages * keep[:, None, None, :, None]
    scale = 1.0 / SAMP

    def one_tile(pair):
        left = clean[pair[0]]
        right = clean[pair[1]]
        prec = lax.Precision.HIGHEST
        real = jnp.einsum("cps,cqs->cpq", left[:, 0], right[:, 0], precision=prec) + jnp.einsum("cps,cqs->cpq", left[:, 1], right[:, 1], precision=prec)
        imag = jnp.einsum("cps,cqs->cpq", left[:, 1], right[:, 0], precision=prec) - jnp.einsum("cps,cqs->cpq", left[:, 0], right[:, 1], precision=prec)
        return jnp.stack([real, imag], axis=1) * scale

    return lax.map(one_tile, pair_table)
```

```python
import functools

import jax
import jax.numpy as jnp
from jax import lax
from jax.experimental import pallas as pl
from jax.experimental.pallas import tpu as pltpu
from jax.sharding import PartitionSpec as P


def passed_along(value, axis):
    count = lax.axis_size(axis)
    pairs = [(source, (source - 1) % count) for source in range(count)]
    return lax.ppermute(value, axis, pairs)


def turned(value):
    return lax.all_to_all(value, "freq", split_axis=0, concat_axis=0, tiled=True)


def tiles_kernel(start, count, chan0, steps, n_sets, has_prev, slots_ref, *refs):
    sets = refs[:n_sets]
    out_ref, hi, lo, stage, sems = refs[n_sets + has_prev :]
    step = pl.program_id(0)
    slot = lax.rem(step, 2)
    groups, per_dev, _, rows, samples = sets[0].shape
    width = groups * rows
    scale = 1.0 / samples

    def copy_out(which, channel):
        return pltpu.make_async_copy(
            stage.at[which],
            out_ref.at[pl.ds(start, count), chan0 + channel],
            sems.at[which],
        )

    for index, ref in enumerate(sets):
        for block in range(per_dev):
            at = index * per_dev + block
            re = ref[:, block, 0].reshape(width, samples)
            im = ref[:, block, 1].reshape(width, samples)
            re_hi = re.astype(jnp.bfloat16)
            im_hi = im.astype(jnp.bfloat16)
            re_rest = re - re_hi.astype(jnp.float32)
            im_rest = im - im_hi.astype(jnp.float32)
            for held, real, imag, minus in (
                (hi, re_hi, im_hi, (-im).astype(jnp.bfloat16)),
                (
                    lo,
                    re_rest.astype(jnp.bfloat16),
                    im_rest.astype(jnp.bfloat16),
                    (-im_rest).astype(jnp.bfloat16),
                ),
            ):
                held[at, :width, :samples] = real
                held[at, :width, samples:] = imag
                held[at, width:, :samples] = minus
                held[at, width:, samples:] = real

    if steps > 2:

        @pl.when(step >= 2)
        def _():
            copy_out(slot, step - 2).wait()

    def dot(a, b):
        return lax.dot_general(
            a, b, (((1,), (1,)), ((), ())), preferred_element_type=jnp.float32
        )

    def tile(index, carry):
        x = slots_ref[2 * (start + index)]
        y = slots_ref[2 * (start + index) + 1]
        x_hi = hi[x, :width, :]
        x_lo = lo[x, :width, :]
        y_hi = hi[y]
        y_lo = lo[y]
        total = (dot(x_lo, y_hi) + dot(x_hi, y_lo) + dot(x_hi, y_hi)) * scale
        stage[slot, index, 0] = total[:, :width]
        stage[slot, index, 1] = total[:, width:]
        return carry

    lax.fori_loop(0, count, tile, 0, unroll=2 if count % 2 == 0 else 1)
    copy_out(slot, step).start()

    @pl.when(step == steps - 1)
    def _():
        if steps > 1:
            copy_out(lax.rem(step + 1, 2), step - 1).wait()
        copy_out(slot, step).wait()


def place_group(prev, out_type, slots, start, count, chan0, sets):
    groups, per_dev, steps, _, rows, samples = sets[0].shape
    width = groups * rows
    n_sets = len(sets)
    has_prev = 0 if prev is None else 1
    spec = pl.BlockSpec(
        (groups, per_dev, None, 2, rows, samples), lambda c, *_: (0, 0, c, 0, 0, 0)
    )
    any_spec = pl.BlockSpec(memory_space=pl.ANY)
    flops = 3 * 2 * 2 * width * width * 2 * samples * count * steps
    moved = 4 * (sum(one.size for one in sets) + 2 * width * width * count * steps)
    call = pl.pallas_call(
        functools.partial(tiles_kernel, start, count, chan0, steps, n_sets, has_prev),
        out_shape=out_type,
        grid_spec=pltpu.PrefetchScalarGridSpec(
            num_scalar_prefetch=1,
            grid=(steps,),
            in_specs=[spec] * n_sets + [any_spec] * has_prev,
            out_specs=any_spec,
            scratch_shapes=[
                pltpu.VMEM((n_sets * per_dev, 2 * width, 2 * samples), jnp.bfloat16),
                pltpu.VMEM((n_sets * per_dev, 2 * width, 2 * samples), jnp.bfloat16),
                pltpu.VMEM((2, count, 2, width, width), jnp.float32),
                pltpu.SemaphoreType.DMA((2,)),
            ],
        ),
        input_output_aliases={1 + n_sets: 0} if has_prev else {},
        compiler_params=pltpu.CompilerParams(
            dimension_semantics=("arbitrary",), vmem_limit_bytes=32 * 1024 * 1024
        ),
        cost_estimate=pl.CostEstimate(
            flops=flops, bytes_accessed=moved, transcendentals=0
        ),
    )
    return call(slots, *sets, *([prev] if has_prev else []))


def shards(voltages, pair_table, bad_feeds):
    blk_count = lax.axis_size("blk")
    freq_count = lax.axis_size("freq")
    here = lax.axis_index("blk")
    per_dev, chans, _, rows, samples = voltages.shape
    width = rows * freq_count
    chan_dev = chans // freq_count
    half = blk_count // 2
    chunks = 4 if per_dev > 1 and chan_dev % 4 == 0 else 1
    per_chunk = chan_dev // chunks
    tile_count = per_dev * per_dev
    own_count = per_dev * (per_dev + 1) // 2
    shared_count = (tile_count + 1) // 2

    blocks = here * per_dev + jnp.arange(per_dev, dtype=jnp.int32)
    places = lax.axis_index("freq") * rows + jnp.arange(rows, dtype=jnp.int32)
    inputs = blocks[:, None] * width + places[None, :]
    flagged = jnp.any((inputs // 2)[:, :, None] == bad_feeds[None, None, :], axis=-1)
    keep = jnp.where(flagged, 0.0, 1.0).astype(jnp.float32)
    slots = jnp.where(
        pair_table // per_dev == here, pair_table % per_dev, per_dev + pair_table % per_dev
    ).reshape(-1)

    split = voltages.reshape(per_dev, freq_count, chunks, per_chunk, 2, rows, samples)
    raw = [
        jnp.swapaxes(split[:, :, g], 0, 1) * keep[None, :, None, None, :, None]
        for g in range(chunks)
    ]
    early = passed_along(raw[-1], "blk") if chunks > 1 else None
    own = [turned(piece) for piece in raw]

    out_type = jax.ShapeDtypeStruct(
        (pair_table.shape[0], chan_dev, 2, width, width), jnp.float32
    )
    visibility = None
    for g in range(chunks):
        visibility = place_group(
            visibility, out_type, slots, 0, own_count, g * per_chunk, [own[g]]
        )
    far = own
    for step in range(1, half + 1):
        far = [
            turned(early)
            if step == 1 and early is not None and g == chunks - 1
            else passed_along(far[g], "blk")
            for g in range(chunks)
        ]
        for g in range(chunks):
            visibility = place_group(
                visibility,
                out_type,
                slots,
                own_count + (step - 1) * tile_count,
                tile_count if step < half else shared_count,
                g * per_chunk,
                [own[g], far[g]],
            )
    return visibility


def solution(mesh):
    placed = (P("blk", None, None, "freq", None), P("blk", None), P())
    return jax.shard_map(
        shards,
        mesh=mesh,
        in_specs=placed,
        out_specs=P("blk", "freq", None, None, None),
        check_vma=False,
    )
```

```python
import functools

import jax
import jax.numpy as jnp
from jax import lax
from jax.experimental import pallas as pl
from jax.experimental.pallas import tpu as pltpu
from jax.sharding import PartitionSpec as P


def passed_along(value, axis):
    count = lax.axis_size(axis)
    pairs = [(source, (source - 1) % count) for source in range(count)]
    return lax.ppermute(value, axis, pairs)


def turn_kernel(chunks, volts, *refs):
    own = refs[:chunks]
    far = refs[chunks : 2 * chunks - 1]
    local_sem, send_sem, recv_sem, pass_send, pass_recv = refs[2 * chunks - 1 :]
    count = lax.axis_size("freq")
    me = lax.axis_index("freq")
    blk_count = lax.axis_size("blk")
    here = lax.axis_index("blk")
    before = lax.rem(here + blk_count - 1, blk_count)
    after = lax.rem(here + 1, blk_count)
    chan_dev = volts.shape[1] // count
    per_chunk = chan_dev // chunks

    barrier = pltpu.get_barrier_semaphore()
    for shift in range(1, count):
        pl.semaphore_signal(
            barrier,
            inc=1,
            device_id=(lax.rem(me + shift, count), here),
            device_id_type=pl.DeviceIdType.MESH,
        )
    for other in (before, after):
        pl.semaphore_signal(
            barrier, inc=1, device_id=(me, other), device_id_type=pl.DeviceIdType.MESH
        )
    pl.semaphore_wait(barrier, count + 1)

    def part(device, g):
        return volts.at[:, pl.ds(device * chan_dev + g * per_chunk, per_chunk)]

    kept, sent, passed = [], [], []
    for g in range(chunks):
        kept.append(pltpu.make_async_copy(part(me, g), own[g].at[me], local_sem.at[g]))
        kept[g].start()
        sent.append([])
        for shift in range(1, count):
            peer = lax.rem(me + shift, count)
            copy = pltpu.make_async_remote_copy(
                src_ref=part(peer, g),
                dst_ref=own[g].at[me],
                send_sem=send_sem.at[g, shift - 1],
                recv_sem=recv_sem.at[g, shift - 1],
                device_id=(peer, here),
                device_id_type=pl.DeviceIdType.MESH,
            )
            copy.start()
            sent[g].append(copy)
    for g in range(chunks):
        kept[g].wait()
        for copy in sent[g]:
            copy.wait_recv()
        if g < chunks - 1:
            copy = pltpu.make_async_remote_copy(
                src_ref=own[g],
                dst_ref=far[g],
                send_sem=pass_send.at[g],
                recv_sem=pass_recv.at[g],
                device_id=(me, before),
                device_id_type=pl.DeviceIdType.MESH,
            )
            copy.start()
            passed.append(copy)
    for g in range(chunks):
        for copy in sent[g]:
            copy.wait_send()
    for copy in passed:
        copy.wait()


def turned(voltages, chunks):
    count = lax.axis_size("freq")
    per_dev, chans, _, rows, samples = voltages.shape
    per_chunk = chans // count // chunks
    piece = jax.ShapeDtypeStruct(
        (count, per_dev, per_chunk, 2, rows, samples), voltages.dtype
    )
    any_spec = pl.BlockSpec(memory_space=pl.ANY)
    made = 2 * chunks - 1
    outs = pl.pallas_call(
        functools.partial(turn_kernel, chunks),
        out_shape=[piece] * made,
        in_specs=[any_spec],
        out_specs=[any_spec] * made,
        scratch_shapes=[
            pltpu.SemaphoreType.DMA((chunks,)),
            pltpu.SemaphoreType.DMA((chunks, count - 1)),
            pltpu.SemaphoreType.DMA((chunks, count - 1)),
            pltpu.SemaphoreType.DMA((chunks,)),
            pltpu.SemaphoreType.DMA((chunks,)),
        ],
        compiler_params=pltpu.CompilerParams(collective_id=0, has_side_effects=True),
        cost_estimate=pl.CostEstimate(
            flops=0, bytes_accessed=8 * voltages.size, transcendentals=0
        ),
    )(voltages)
    return list(outs[:chunks]), list(outs[chunks:])


def tiles_kernel(start, count, chan0, steps, n_sets, has_prev, slots_ref, *refs):
    sets = refs[:n_sets]
    keep_ref = refs[n_sets]
    out_ref, left, right_hi, right_lo, stage, sems = refs[n_sets + 1 + has_prev :]
    step = pl.program_id(0)
    slot = lax.rem(step, 2)
    groups, per_dev, _, rows, samples = sets[0].shape
    width = groups * rows
    scale = 1.0 / samples

    def copy_out(which, channel):
        return pltpu.make_async_copy(
            stage.at[which],
            out_ref.at[pl.ds(start, count), chan0 + channel],
            sems.at[which],
        )

    def halves(value):
        head = value.astype(jnp.bfloat16)
        return head, (value - head.astype(jnp.float32)).astype(jnp.bfloat16)

    for index, ref in enumerate(sets):
        for block in range(per_dev):
            at = index * per_dev + block
            keep = keep_ref[at]
            re = ref[:, block, 0].reshape(width, samples) * keep
            im = ref[:, block, 1].reshape(width, samples) * keep
            for column, value in ((0, re), (samples, im)):
                head, tail = halves(value)
                left[at, :width, column : column + samples] = head
                left[at, width:, column : column + samples] = tail
            re = re.T
            im = im.T
            for row, column, value in (
                (0, 0, re),
                (samples, 0, im),
                (0, width, -im),
                (samples, width, re),
            ):
                head, tail = halves(value)
                right_hi[at, row : row + samples, column : column + width] = head
                right_lo[at, row : row + samples, column : column + width] = tail

    if steps > 2:

        @pl.when(step >= 2)
        def _():
            copy_out(slot, step - 2).wait()

    def dot(a, b):
        return jnp.dot(a, b, preferred_element_type=jnp.float32)

    def tile(index, carry):
        x = slots_ref[2 * (start + index)]
        y = slots_ref[2 * (start + index) + 1]
        by_head = dot(left[x], right_hi[y])
        by_tail = dot(left[x, :width, :], right_lo[y])
        total = (by_head[width:] + by_tail + by_head[:width]) * scale
        stage[slot, index, 0] = total[:, :width]
        stage[slot, index, 1] = total[:, width:]
        return carry

    lax.fori_loop(0, count, tile, 0, unroll=2 if count % 2 == 0 else 1)
    copy_out(slot, step).start()

    @pl.when(step == steps - 1)
    def _():
        if steps > 1:
            copy_out(lax.rem(step + 1, 2), step - 1).wait()
        copy_out(slot, step).wait()


def place_group(prev, out_type, slots, start, count, chan0, sets, keep):
    groups, per_dev, steps, _, rows, samples = sets[0].shape
    width = groups * rows
    n_sets = len(sets)
    has_prev = 0 if prev is None else 1
    spec = pl.BlockSpec(
        (groups, per_dev, None, 2, rows, samples), lambda c, *_: (0, 0, c, 0, 0, 0)
    )
    any_spec = pl.BlockSpec(memory_space=pl.ANY)
    flops = 3 * 3 * 2 * 2 * width * width * 2 * samples * count * steps
    moved = 4 * (sum(one.size for one in sets) + 2 * width * width * count * steps)
    call = pl.pallas_call(
        functools.partial(tiles_kernel, start, count, chan0, steps, n_sets, has_prev),
        out_shape=out_type,
        grid_spec=pltpu.PrefetchScalarGridSpec(
            num_scalar_prefetch=1,
            grid=(steps,),
            in_specs=[spec] * n_sets
            + [pl.BlockSpec(keep.shape, lambda c, *_: (0, 0, 0))]
            + [any_spec] * has_prev,
            out_specs=any_spec,
            scratch_shapes=[
                pltpu.VMEM((n_sets * per_dev, 2 * width, 2 * samples), jnp.bfloat16),
                pltpu.VMEM((n_sets * per_dev, 2 * samples, 2 * width), jnp.bfloat16),
                pltpu.VMEM((n_sets * per_dev, 2 * samples, 2 * width), jnp.bfloat16),
                pltpu.VMEM((2, count, 2, width, width), jnp.float32),
                pltpu.SemaphoreType.DMA((2,)),
            ],
        ),
        input_output_aliases={2 + n_sets: 0} if has_prev else {},
        compiler_params=pltpu.CompilerParams(
            dimension_semantics=("arbitrary",), vmem_limit_bytes=32 * 1024 * 1024
        ),
        cost_estimate=pl.CostEstimate(
            flops=flops, bytes_accessed=moved, transcendentals=0
        ),
    )
    return call(slots, *sets, keep, *([prev] if has_prev else []))


def shards(voltages, pair_table, bad_feeds):
    blk_count = lax.axis_size("blk")
    freq_count = lax.axis_size("freq")
    here = lax.axis_index("blk")
    per_dev, chans, _, rows, samples = voltages.shape
    width = rows * freq_count
    chan_dev = chans // freq_count
    half = blk_count // 2
    chunks = 4 if per_dev > 1 and chan_dev % 4 == 0 else 1
    per_chunk = chan_dev // chunks
    tile_count = per_dev * per_dev
    own_count = per_dev * (per_dev + 1) // 2
    shared_count = (tile_count + 1) // 2

    def kept(step):
        first = lax.rem(here + step, blk_count) * per_dev * width
        inputs = first + jnp.arange(per_dev * width, dtype=jnp.int32)
        flagged = jnp.any((inputs // 2)[:, None] == bad_feeds[None, :], axis=-1)
        return jnp.where(flagged, 0.0, 1.0).astype(jnp.float32).reshape(per_dev, width, 1)

    slots = jnp.where(
        pair_table // per_dev == here, pair_table % per_dev, per_dev + pair_table % per_dev
    ).reshape(-1)

    own, first_hop = turned(voltages, chunks)
    own_keep = kept(0)

    out_type = jax.ShapeDtypeStruct(
        (pair_table.shape[0], chan_dev, 2, width, width), jnp.float32
    )
    visibility = None
    for g in range(chunks):
        visibility = place_group(
            visibility, out_type, slots, 0, own_count, g * per_chunk, [own[g]], own_keep
        )
    far = own
    for step in range(1, half + 1):
        far = [
            first_hop[g] if step == 1 and g < chunks - 1 else passed_along(far[g], "blk")
            for g in range(chunks)
        ]
        both_keep = jnp.concatenate([own_keep, kept(step)], axis=0)
        for g in range(chunks):
            visibility = place_group(
                visibility,
                out_type,
                slots,
                own_count + (step - 1) * tile_count,
                tile_count if step < half else shared_count,
                g * per_chunk,
                [own[g], far[g]],
                both_keep,
            )
    return visibility


def solution(mesh):
    placed = (P("blk", None, None, "freq", None), P("blk", None), P())
    return jax.shard_map(
        shards,
        mesh=mesh,
        in_specs=placed,
        out_specs=P("blk", "freq", None, None, None),
        check_vma=False,
    )
```

```python
import functools

import jax
import jax.numpy as jnp
from jax import lax
from jax.experimental import pallas as pl
from jax.experimental.pallas import tpu as pltpu
from jax.sharding import PartitionSpec as P


def passed_along(value, axis):
    count = lax.axis_size(axis)
    pairs = [(source, (source - 1) % count) for source in range(count)]
    return lax.ppermute(value, axis, pairs)


def turn_kernel(chunks, volts, *refs):
    own = refs[:chunks]
    far = refs[chunks : 2 * chunks]
    local_sem, send_sem, recv_sem, pass_send, pass_recv = refs[2 * chunks :]
    count = lax.axis_size("freq")
    me = lax.axis_index("freq")
    blk_count = lax.axis_size("blk")
    here = lax.axis_index("blk")
    before = lax.rem(here + blk_count - 1, blk_count)
    after = lax.rem(here + 1, blk_count)
    chan_dev = volts.shape[1] // count
    per_chunk = chan_dev // chunks

    barrier = pltpu.get_barrier_semaphore()
    for shift in range(1, count):
        pl.semaphore_signal(
            barrier,
            inc=1,
            device_id=(lax.rem(me + shift, count), here),
            device_id_type=pl.DeviceIdType.MESH,
        )
    for other in (before, after):
        pl.semaphore_signal(
            barrier, inc=1, device_id=(me, other), device_id_type=pl.DeviceIdType.MESH
        )
    pl.semaphore_wait(barrier, count + 1)

    def begin(unit):
        held = own[unit // per_chunk].at[me, :, unit % per_chunk]
        kept = pltpu.make_async_copy(
            volts.at[:, me * chan_dev + unit], held, local_sem.at[unit]
        )
        sent = []
        for shift in range(1, count):
            peer = lax.rem(me + shift, count)
            copy = pltpu.make_async_remote_copy(
                src_ref=volts.at[:, peer * chan_dev + unit],
                dst_ref=held,
                send_sem=send_sem.at[unit, shift - 1],
                recv_sem=recv_sem.at[unit, shift - 1],
                device_id=(peer, here),
                device_id_type=pl.DeviceIdType.MESH,
            )
            copy.start()
            sent.append(copy)
        kept.start()
        return kept, sent

    passed = []
    kept, sent = begin(0)
    for unit in range(chan_dev):
        for copy in sent:
            copy.wait_send()
        now_kept, now_sent = kept, sent
        if unit + 1 < chan_dev:
            kept, sent = begin(unit + 1)
        now_kept.wait()
        for copy in now_sent:
            copy.wait_recv()
        copy = pltpu.make_async_remote_copy(
            src_ref=own[unit // per_chunk].at[:, :, unit % per_chunk],
            dst_ref=far[unit // per_chunk].at[:, :, unit % per_chunk],
            send_sem=pass_send.at[unit],
            recv_sem=pass_recv.at[unit],
            device_id=(me, before),
            device_id_type=pl.DeviceIdType.MESH,
        )
        copy.start()
        passed.append(copy)
    for copy in passed:
        copy.wait()


def turned(voltages, chunks):
    count = lax.axis_size("freq")
    per_dev, chans, _, rows, samples = voltages.shape
    chan_dev = chans // count
    per_chunk = chan_dev // chunks
    piece = jax.ShapeDtypeStruct(
        (count, per_dev, per_chunk, 2, rows, samples), voltages.dtype
    )
    any_spec = pl.BlockSpec(memory_space=pl.ANY)
    made = 2 * chunks
    outs = pl.pallas_call(
        functools.partial(turn_kernel, chunks),
        out_shape=[piece] * made,
        in_specs=[any_spec],
        out_specs=[any_spec] * made,
        scratch_shapes=[
            pltpu.SemaphoreType.DMA((chan_dev,)),
            pltpu.SemaphoreType.DMA((chan_dev, count - 1)),
            pltpu.SemaphoreType.DMA((chan_dev, count - 1)),
            pltpu.SemaphoreType.DMA((chan_dev,)),
            pltpu.SemaphoreType.DMA((chan_dev,)),
        ],
        compiler_params=pltpu.CompilerParams(collective_id=0, has_side_effects=True),
        cost_estimate=pl.CostEstimate(
            flops=0, bytes_accessed=8 * voltages.size, transcendentals=0
        ),
    )(voltages)
    return list(outs[:chunks]), list(outs[chunks:])


def tiles_kernel(start, count, chan0, steps, n_sets, has_prev, slots_ref, *refs):
    sets = refs[:n_sets]
    keep_ref = refs[n_sets]
    out_ref, left, right_hi, right_lo, stage, sems = refs[n_sets + 1 + has_prev :]
    step = pl.program_id(0)
    slot = lax.rem(step, 2)
    groups, per_dev, _, rows, samples = sets[0].shape
    width = groups * rows
    scale = 1.0 / samples

    def copy_out(which, channel):
        return pltpu.make_async_copy(
            stage.at[which],
            out_ref.at[pl.ds(start, count), chan0 + channel],
            sems.at[which],
        )

    def halves(value):
        head = value.astype(jnp.bfloat16)
        return head, (value - head.astype(jnp.float32)).astype(jnp.bfloat16)

    for index, ref in enumerate(sets):
        for block in range(per_dev):
            at = index * per_dev + block
            keep = keep_ref[at]
            re = ref[:, block, 0].reshape(width, samples) * keep
            im = ref[:, block, 1].reshape(width, samples) * keep
            for column, value in ((0, re), (samples, im)):
                head, tail = halves(value)
                left[at, :width, column : column + samples] = head
                left[at, width:, column : column + samples] = tail
            re = re.T
            im = im.T
            for row, column, value in (
                (0, 0, re),
                (samples, 0, im),
                (0, width, -im),
                (samples, width, re),
            ):
                head, tail = halves(value)
                right_hi[at, row : row + samples, column : column + width] = head
                right_lo[at, row : row + samples, column : column + width] = tail

    if steps > 2:

        @pl.when(step >= 2)
        def _():
            copy_out(slot, step - 2).wait()

    def dot(a, b):
        return jnp.dot(a, b, preferred_element_type=jnp.float32)

    def tile(index, carry):
        x = slots_ref[2 * (start + index)]
        y = slots_ref[2 * (start + index) + 1]
        by_head = dot(left[x], right_hi[y])
        by_tail = dot(left[x, :width, :], right_lo[y])
        total = (by_head[width:] + by_tail + by_head[:width]) * scale
        stage[slot, index, 0] = total[:, :width]
        stage[slot, index, 1] = total[:, width:]
        return carry

    lax.fori_loop(0, count, tile, 0, unroll=2 if count % 2 == 0 else 1)
    copy_out(slot, step).start()

    @pl.when(step == steps - 1)
    def _():
        if steps > 1:
            copy_out(lax.rem(step + 1, 2), step - 1).wait()
        copy_out(slot, step).wait()


def place_group(prev, out_type, slots, start, count, chan0, sets, keep):
    groups, per_dev, steps, _, rows, samples = sets[0].shape
    width = groups * rows
    n_sets = len(sets)
    has_prev = 0 if prev is None else 1
    spec = pl.BlockSpec(
        (groups, per_dev, None, 2, rows, samples), lambda c, *_: (0, 0, c, 0, 0, 0)
    )
    any_spec = pl.BlockSpec(memory_space=pl.ANY)
    flops = 3 * 3 * 2 * 2 * width * width * 2 * samples * count * steps
    moved = 4 * (sum(one.size for one in sets) + 2 * width * width * count * steps)
    call = pl.pallas_call(
        functools.partial(tiles_kernel, start, count, chan0, steps, n_sets, has_prev),
        out_shape=out_type,
        grid_spec=pltpu.PrefetchScalarGridSpec(
            num_scalar_prefetch=1,
            grid=(steps,),
            in_specs=[spec] * n_sets
            + [pl.BlockSpec(keep.shape, lambda c, *_: (0, 0, 0))]
            + [any_spec] * has_prev,
            out_specs=any_spec,
            scratch_shapes=[
                pltpu.VMEM((n_sets * per_dev, 2 * width, 2 * samples), jnp.bfloat16),
                pltpu.VMEM((n_sets * per_dev, 2 * samples, 2 * width), jnp.bfloat16),
                pltpu.VMEM((n_sets * per_dev, 2 * samples, 2 * width), jnp.bfloat16),
                pltpu.VMEM((2, count, 2, width, width), jnp.float32),
                pltpu.SemaphoreType.DMA((2,)),
            ],
        ),
        input_output_aliases={2 + n_sets: 0} if has_prev else {},
        compiler_params=pltpu.CompilerParams(
            dimension_semantics=("arbitrary",), vmem_limit_bytes=32 * 1024 * 1024
        ),
        cost_estimate=pl.CostEstimate(
            flops=flops, bytes_accessed=moved, transcendentals=0
        ),
    )
    return call(slots, *sets, keep, *([prev] if has_prev else []))


def shards(voltages, pair_table, bad_feeds):
    blk_count = lax.axis_size("blk")
    freq_count = lax.axis_size("freq")
    here = lax.axis_index("blk")
    per_dev, chans, _, rows, samples = voltages.shape
    width = rows * freq_count
    chan_dev = chans // freq_count
    half = blk_count // 2
    chunks = 4 if per_dev > 1 and chan_dev % 4 == 0 else 1
    per_chunk = chan_dev // chunks
    tile_count = per_dev * per_dev
    own_count = per_dev * (per_dev + 1) // 2
    shared_count = (tile_count + 1) // 2

    def kept(step):
        first = lax.rem(here + step, blk_count) * per_dev * width
        inputs = first + jnp.arange(per_dev * width, dtype=jnp.int32)
        flagged = jnp.any((inputs // 2)[:, None] == bad_feeds[None, :], axis=-1)
        return jnp.where(flagged, 0.0, 1.0).astype(jnp.float32).reshape(per_dev, width, 1)

    slots = jnp.where(
        pair_table // per_dev == here, pair_table % per_dev, per_dev + pair_table % per_dev
    ).reshape(-1)

    own, first_hop = turned(voltages, chunks)
    own_keep = kept(0)

    out_type = jax.ShapeDtypeStruct(
        (pair_table.shape[0], chan_dev, 2, width, width), jnp.float32
    )
    visibility = None
    for g in range(chunks):
        visibility = place_group(
            visibility, out_type, slots, 0, own_count, g * per_chunk, [own[g]], own_keep
        )
    for step in range(1, half + 1):
        far = first_hop if step == 1 else [passed_along(piece, "blk") for piece in far]
        both_keep = jnp.concatenate([own_keep, kept(step)], axis=0)
        for g in range(chunks):
            visibility = place_group(
                visibility,
                out_type,
                slots,
                own_count + (step - 1) * tile_count,
                tile_count if step < half else shared_count,
                g * per_chunk,
                [own[g], far[g]],
                both_keep,
            )
    return visibility


def solution(mesh):
    placed = (P("blk", None, None, "freq", None), P("blk", None), P())
    return jax.shard_map(
        shards,
        mesh=mesh,
        in_specs=placed,
        out_specs=P("blk", "freq", None, None, None),
        check_vma=False,
    )
```
